32 devices in a mesh: row: 8 (over y, x, core), col: 4 (over z).
Axes of the slice: x: 2, y: 2, z: 4, core: 2. Of those that a mesh axis runs over, the one named last changes fastest.
Arguments:
- tokens: bfloat16 [8, 4, 736, 1024], P('row', 'col'), may hold values from -6 to 6
- local_params: bfloat16 [8, 4, 2, 1024, 1024], P('row', 'col'), may hold values from -0.1875 to 0.1875
- outer_params: float32 [2, 4, 4, 8, 32, 1024], P(None, None, 'col', 'row'), may hold values from -0.1875 to 0.1875
- momentum: float32 [2, 4, 4, 8, 32, 1024], P(None, None, 'col', 'row'), may hold values from -0.1875 to 0.1875
- table: int32 [8, 4], replicated, may hold values from 0 to 3, each once within a row
- counts: int32 [8, 4], replicated, may hold values from 64 to 4095
Outputs:
- path_params: bfloat16 [8, 4, 2, 1024, 1024], P('row', 'col')
- outer_out: float32 [2, 4, 4, 8, 32, 1024], P(None, None, 'col', 'row')
- momentum_out: float32 [2, 4, 4, 8, 32, 1024], P(None, None, 'col', 'row')
- hidden_out: bfloat16 [8, 4, 736, 1024], P('row', 'col')
The draws below stay inside these ranges and needn't reach their ends.
Inputs may be any that keep to these rules, and one draw needn't show every extreme that they name: Each row of the table names every level-two module exactly once.
All inputs are finite; a program needn't handle non-finite values.
Results may differ from the reference program's by a relative error of at most 0.01.
Values may be sent and summed in bfloat16 or wider, within the bound.
A program may use at most 64 MiB of HBM per device.

```python
import jax
import jax.numpy as jnp
from jax import lax

D = 1024
LAYERS = 2
TOK_DEV = 736
MODULES = 4
ROWS_PIECE = 32
N_ROW = 8
N_COL = 4


def place_ends(entries, stream_key, smallest, largest):
    shape = entries.shape
    index_at = [jax.random.randint(jax.random.fold_in(stream_key, axis), (), 0, shape[axis]) for axis in range(len(shape))]
    entries = entries.at[tuple(index_at)].set(smallest)
    longest = shape.index(max(shape))
    index_at[longest] = (index_at[longest] + 1) % shape[longest]
    return entries.at[tuple(index_at)].set(largest)


def block_levels(rng, extent, split, smallest, high):
    loudness = 1.0
    for position, blocks in split:
        heights = jax.random.uniform(jax.random.fold_in(jax.random.fold_in(rng, 6), position), (blocks,), jnp.float32, smallest / len(split), high / len(split))
        loudness = loudness * jnp.repeat(jnp.exp(heights), extent[position] // blocks).reshape((-1,) + (1,) * (len(extent) - 1 - position))
    return loudness


def bell_draw(key, dims, scale, most, cuts=(), held_as=jnp.bfloat16):
    result = jax.random.normal(key, dims, jnp.float32) * scale
    if len(cuts) > 0:
        result = block_levels(key, dims, cuts, -0.22, 0.18) * result
    return jnp.clip(result, min=-most, max=most).astype(held_as)


def setup_inputs(seed: int = 0) -> dict:
    key_list = jax.random.split(jax.random.key(seed), 7)
    return {
        "tokens": bell_draw(key_list[0], (N_ROW, N_COL, TOK_DEV, D), 1.0, 6.0, ((0, 8), (1, 4))),
        "local_params": bell_draw(key_list[1], (N_ROW, N_COL, LAYERS, D, D), D ** -0.5, 0.1875, ((0, 8), (1, 4))),
        "outer_params": bell_draw(key_list[2], (LAYERS, MODULES, N_COL, N_ROW, ROWS_PIECE, D), D ** -0.5, 0.1875, ((2, 4), (3, 8)), jnp.float32),
        "momentum": bell_draw(key_list[3], (LAYERS, MODULES, N_COL, N_ROW, ROWS_PIECE, D), D ** -0.5, 0.1875, ((2, 4), (3, 8)), jnp.float32),
        "table": jax.vmap(lambda own: jax.random.permutation(own, N_COL))(jax.random.split(key_list[4], N_ROW)).reshape((N_ROW, N_COL)).astype(jnp.int32),
        "counts": place_ends(jax.random.randint(key_list[5], (N_ROW, N_COL), 64, 4096), jax.random.fold_in(key_list[5], 1), 64, 4095).astype(jnp.int32),
    }


def micro_step(tokens_path, params_path):
    state = tokens_path.astype(jnp.float32)
    for layer in range(LAYERS):
        scale = lax.rsqrt(lax.optimization_barrier(jnp.mean(state * state, axis=-1, keepdims=True)) + 1e-06)
        normed = (state * scale).astype(jnp.bfloat16)
        mixed = jnp.dot(normed, params_path[layer], preferred_element_type=jnp.float32)
        state = state + jax.nn.gelu(mixed, approximate=False)
    return state.astype(jnp.bfloat16)

def reference(tokens, local_params, outer_params, momentum, table, counts):
    n_row = table.shape[0]
    n_col = table.shape[1]
    width = local_params.shape[-1]
    layers = local_params.shape[2]
    ids = jnp.arange(n_col, dtype=jnp.int32)
    matches = (table[:, :, None] == ids[None, None, :]).astype(jnp.float32)
    totals = lax.optimization_barrier(jnp.sum(counts.astype(jnp.float32)[:, :, None] * matches, axis=(0, 1)))
    share = counts.astype(jnp.float32) / lax.optimization_barrier(jnp.sum(matches * totals[None, None, :], axis=2))
    slots = jnp.arange(n_col, dtype=jnp.int32)
    inverse = lax.optimization_barrier(jnp.sum(slots[None, :, None] * (table[:, :, None] == ids[None, None, :]).astype(jnp.int32), axis=1)).astype(jnp.int32)

    def add_row(acc, index):
        local_row = local_params[index]
        weights = share[index]
        term = (weights[:, None, None, None] * local_row.astype(jnp.float32)).astype(jnp.bfloat16)
        ordered = jnp.take(term, inverse[index], axis=0)
        return (acc + jnp.transpose(ordered.astype(jnp.float32), (1, 0, 2, 3)), None)
    start = jnp.zeros((layers, n_col, width, width), jnp.float32)
    average, unused = lax.scan(add_row, start, jnp.arange(n_row, dtype=jnp.int32))
    outer = outer_params.reshape(layers, n_col, width, width)
    moment = momentum.reshape(layers, n_col, width, width)
    delta = outer - average
    moment_new = 0.9 * moment + delta
    outer_new = outer - 0.7 * (delta + 0.9 * moment_new)
    picked = jnp.take(outer_new.astype(jnp.bfloat16), table, axis=1)
    path_params = jnp.transpose(picked, (1, 2, 0, 3, 4))
    flat_tokens = tokens.reshape(n_row * n_col, tokens.shape[2], width)
    flat_params = local_params.reshape(n_row * n_col, layers, width, width)
    hidden = lax.map(lambda pair: micro_step(pair[0], pair[1]), (flat_tokens, flat_params))
    hidden_out = hidden.reshape(tokens.shape)
    return (path_params, outer_new.reshape(outer_params.shape), moment_new.reshape(momentum.shape), hidden_out)
```

```python
import functools

import jax
import jax.numpy as jnp
from jax import lax
from jax.experimental import pallas as pl
from jax.experimental.pallas import tpu as pltpu
from jax.sharding import PartitionSpec as P

MESH = pl.DeviceIdType.MESH
BLOCK = 256
PARTS = 2
TILE = 192


def round_kernel(
    n_row, n_col, tokens, params, source, outer, moment, table, counts,
    path, outer_new, moment_new, hidden,
    weights, landed, own, z_out, z_in, chosen, state, normed,
    in_send, in_recv, z_send, z_recv, b_send, b_recv, ret_send, ret_recv, here_sem, *spread,
):
    row, col = lax.axis_index("row"), lax.axis_index("col")
    layers, width = params.shape[0], params.shape[2]
    part = width // PARTS
    blocks = part // BLOCK
    chunks = [(layer, p) for layer in range(layers) for p in range(PARTS)]
    n_chunks = len(chunks)

    barrier = pltpu.get_barrier_semaphore()
    for d in range(1, n_row):
        pl.semaphore_signal(barrier, inc=1, device_id=(lax.rem(row + d, n_row), col), device_id_type=MESH)
    for d in range(1, n_col):
        pl.semaphore_signal(barrier, inc=1, device_id=(row, lax.rem(col + d, n_col)), device_id_type=MESH)
    pl.semaphore_wait(barrier, n_row + n_col - 2)

    def cols(k):
        return pl.ds(chunks[k][1] * part, part)

    def in_copy(k, slot_of, to, peer):
        return pltpu.make_async_remote_copy(
            src_ref=source.at[chunks[k][0], :, to, :, cols(k)],
            dst_ref=landed.at[k, slot_of],
            send_sem=in_send.at[k, to],
            recv_sem=in_recv.at[k, slot_of],
            device_id=(peer, col),
            device_id_type=MESH,
        )

    def in_own(k):
        return pltpu.make_async_copy(source.at[chunks[k][0], :, row, :, cols(k)], landed.at[k, row], here_sem.at[0, k])

    def z_copy(k, slot_of, to):
        return pltpu.make_async_remote_copy(
            src_ref=z_out.at[k, to],
            dst_ref=z_in.at[k, slot_of],
            send_sem=z_send.at[k, to],
            recv_sem=z_recv.at[k, slot_of],
            device_id=(row, to),
            device_id_type=MESH,
        )

    def b_copy(k, slot_of, to):
        return pltpu.make_async_remote_copy(
            src_ref=spread[k].at[slot_of],
            dst_ref=spread[k].at[slot_of],
            send_sem=b_send.at[k, to],
            recv_sem=b_recv.at[k, slot_of],
            device_id=(row, to),
            device_id_type=MESH,
        )

    def ret_copy(k, slot_of, to):
        return pltpu.make_async_remote_copy(
            src_ref=chosen.at[k, to],
            dst_ref=path.at[chunks[k][0], :, slot_of, :, cols(k)],
            send_sem=ret_send.at[k, to],
            recv_sem=ret_recv.at[k, slot_of],
            device_id=(to, col),
            device_id_type=MESH,
        )

    def ret_own(k):
        return pltpu.make_async_copy(chosen.at[k, row], path.at[chunks[k][0], :, row, :, cols(k)], here_sem.at[1, k])

    def others(me, n):
        return [lax.rem(me + d, n) for d in range(1, n)]

    for k in range(n_chunks):
        in_own(k).start()
        for to in others(row, n_row):
            in_copy(k, row, to, to).start()

    def fill_weight(i, carry):
        mine = table[i, col]

        def add(at, total):
            r, c = at // n_col, at % n_col
            return total + jnp.where(table[r, c] == mine, counts[r, c], 0)

        total = lax.fori_loop(0, n_row * n_col, add, jnp.int32(0))
        shape = weights.shape[1:]
        weights[i] = jnp.full(shape, counts[i, col].astype(jnp.float32)) / jnp.full(shape, total.astype(jnp.float32))
        return carry

    lax.fori_loop(0, n_row, fill_weight, 0)

    def micro(start, size):
        rows = pl.ds(start, size)
        state[rows] = tokens[rows].astype(jnp.float32)
        for layer in range(layers):
            def norm(b, carry):
                few = pl.ds(pl.multiple_of(start + b * 16, 16), 16)
                value = state[few]
                scale = lax.rsqrt(jnp.mean(value * value, axis=-1, keepdims=True) + 1e-06)
                normed[few] = (value * scale).astype(jnp.bfloat16)
                return carry

            lax.fori_loop(0, size // 16, norm, 0)

            def mix(b, carry):
                at = pl.ds(pl.multiple_of(b * BLOCK, BLOCK), BLOCK)
                mixed = jnp.dot(normed[rows], params[layer, :, at], preferred_element_type=jnp.float32)
                state[rows, at] += 0.5 * mixed * (1.0 + lax.erf(mixed * (0.5**0.5)))
                return carry

            lax.fori_loop(0, width // BLOCK, mix, 0)
        hidden[rows] = state[rows].astype(jnp.bfloat16)

    def reduce(k):
        in_own(k).wait()
        for frm in others(row, n_row):
            in_copy(k, frm, frm, frm).wait_recv()
        for d in [*range(1, n_col), 0]:
            to = lax.rem(col + d, n_col)

            def block(b, carry, d=d, to=to):
                at = pl.ds(pl.multiple_of(b * BLOCK, BLOCK), BLOCK)
                sums = [jnp.zeros((landed.shape[3], BLOCK), jnp.float32) for _ in range(n_col)]
                for i in range(n_row):
                    term = (weights[i] * landed[k, i, to, :, at].astype(jnp.float32)).astype(jnp.bfloat16)
                    term = term.astype(jnp.float32)
                    module = table[i, col]
                    for m in range(n_col):
                        sums[m] += term * jnp.where(module == m, 1.0, 0.0).astype(jnp.float32)
                for m in range(n_col):
                    if d:
                        z_out[k, to, m, :, at] = sums[m].astype(jnp.bfloat16)
                    else:
                        own[k, m, :, at] = sums[m]
                return carry

            lax.fori_loop(0, blocks, block, 0)
            if d:
                z_copy(k, col, to).start()

    def update(k):
        layer, p = chunks[k]
        for frm in others(col, n_col):
            z_copy(k, frm, frm).wait_recv()

        def block(b, carry):
            at = pl.ds(pl.multiple_of(b * BLOCK, BLOCK), BLOCK)
            whole = pl.ds(pl.multiple_of(p * part + b * BLOCK, BLOCK), BLOCK)
            for m in range(n_col):
                average = own[k, m, :, at]
                for frm in others(col, n_col):
                    average += z_in[k, frm, m, :, at].astype(jnp.float32)
                old = outer[layer, m, :, whole]
                delta = old - average
                fresh = 0.9 * moment[layer, m, :, whole] + delta
                new = old - 0.7 * (delta + 0.9 * fresh)
                moment_new[layer, m, :, whole] = fresh
                outer_new[layer, m, :, whole] = new
                spread[k][col, m, :, at] = new.astype(jnp.bfloat16)
            return carry

        lax.fori_loop(0, blocks, block, 0)
        for to in others(col, n_col):
            b_copy(k, col, to).start()

    def give(k):
        for frm in others(col, n_col):
            b_copy(k, frm, frm).wait_recv()

        for d in [*range(1, n_row), 0]:
            to = lax.rem(row + d, n_row)
            module = table[to, col]

            def pick(c, carry, to=to, module=module):
                chosen[k, to, c] = spread[k][c, module]
                return carry

            lax.fori_loop(0, n_col, pick, 0)
            if d:
                ret_copy(k, row, to).start()
            else:
                ret_own(k).start()

    tiles = [(s, min(TILE, tokens.shape[0] - s)) for s in range(0, tokens.shape[0], TILE)]
    for step in range(max(n_chunks + 2, len(tiles))):
        if step < len(tiles):
            micro(*tiles[step])
        if 2 <= step < n_chunks + 2:
            give(step - 2)
        if 1 <= step < n_chunks + 1:
            update(step - 1)
        if step < n_chunks:
            reduce(step)

    for k in range(n_chunks):
        ret_own(k).wait()
        for at in others(row, n_row):
            ret_copy(k, at, at).wait_recv()
            in_copy(k, row, at, at).wait_send()
            ret_copy(k, row, at).wait_send()
        for at in others(col, n_col):
            z_copy(k, col, at).wait_send()
            b_copy(k, col, at).wait_send()


def with_kernel(tokens, params, outer, moment, table, counts):
    n_row, n_col = table.shape
    layers, width = params.shape[0], params.shape[-1]
    piece = outer.shape[2]
    part = width // PARTS
    n_chunks = layers * PARTS
    source = params.reshape(layers, n_col, n_row, piece, width)
    vmem = pl.BlockSpec(memory_space=pltpu.VMEM)
    smem = pl.BlockSpec(memory_space=pltpu.SMEM)
    hbm = pl.BlockSpec(memory_space=pl.ANY)
    n_tokens = tokens.shape[0]
    flops = 2 * layers * n_tokens * width * width
    return pl.pallas_call(
        functools.partial(round_kernel, n_row, n_col),
        out_shape=(
            jax.ShapeDtypeStruct(source.shape, jnp.bfloat16),
            jax.ShapeDtypeStruct(outer.shape, jnp.float32),
            jax.ShapeDtypeStruct(outer.shape, jnp.float32),
            jax.ShapeDtypeStruct(tokens.shape, jnp.bfloat16),
        ),
        in_specs=[vmem, vmem, hbm, vmem, vmem, smem, smem],
        out_specs=(hbm, vmem, vmem, vmem),
        scratch_shapes=[
            pltpu.VMEM((n_row, 1, BLOCK), jnp.float32),
            pltpu.VMEM((n_chunks, n_row, n_col, piece, part), jnp.bfloat16),
            pltpu.VMEM((n_chunks, n_col, piece, part), jnp.float32),
            pltpu.VMEM((n_chunks, n_col, n_col, piece, part), jnp.bfloat16),
            pltpu.VMEM((n_chunks, n_col, n_col, piece, part), jnp.bfloat16),
            pltpu.VMEM((n_chunks, n_row, n_col, piece, part), jnp.bfloat16),
            pltpu.VMEM((n_tokens, width), jnp.float32),
            pltpu.VMEM((n_tokens, width), jnp.bfloat16),
            pltpu.SemaphoreType.DMA((n_chunks, n_row)),
            pltpu.SemaphoreType.DMA((n_chunks, n_row)),
            pltpu.SemaphoreType.DMA((n_chunks, n_col)),
            pltpu.SemaphoreType.DMA((n_chunks, n_col)),
            pltpu.SemaphoreType.DMA((n_chunks, n_col)),
            pltpu.SemaphoreType.DMA((n_chunks, n_col)),
            pltpu.SemaphoreType.DMA((n_chunks, n_row)),
            pltpu.SemaphoreType.DMA((n_chunks, n_row)),
            pltpu.SemaphoreType.DMA((2, n_chunks)),
            *[pltpu.VMEM((n_col, n_col, piece, part), jnp.bfloat16) for _ in range(n_chunks)],
        ],
        compiler_params=pltpu.CompilerParams(
            collective_id=0, has_side_effects=True, vmem_limit_bytes=52 * 1024 * 1024
        ),
        cost_estimate=pl.CostEstimate(flops=flops, bytes_accessed=20 * 2**20, transcendentals=0),
    )(tokens, params, source, outer, moment, table, counts)


def pick_along(array, index, axis):
    parts = [lax.dynamic_index_in_dim(array, index[m], axis) for m in range(index.shape[0])]
    return jnp.concatenate(parts, axis=axis)


def with_collectives(tokens, params, outer, moment, table, counts):
    n_row, n_col = table.shape
    layers, width = params.shape[0], params.shape[-1]
    ids = jnp.arange(n_col, dtype=jnp.int32)
    matches = (table[:, :, None] == ids[None, None, :]).astype(jnp.float32)
    totals = jnp.sum(counts.astype(jnp.float32)[:, :, None] * matches, axis=(0, 1))
    my_row = lax.dynamic_index_in_dim(table, lax.axis_index("row"), 0, keepdims=False)
    count_row = lax.dynamic_index_in_dim(counts, lax.axis_index("row"), 0, keepdims=False)
    my_module = lax.dynamic_index_in_dim(my_row, lax.axis_index("col"), 0, keepdims=False)
    my_count = lax.dynamic_index_in_dim(count_row, lax.axis_index("col"), 0, keepdims=False)
    share = my_count.astype(jnp.float32) / jnp.sum(totals * (ids == my_module).astype(jnp.float32))
    inverse = jnp.sum(ids[:, None] * (my_row[:, None] == ids[None, :]).astype(jnp.int32), axis=0)
    scaled = (share * params.astype(jnp.float32)).astype(jnp.bfloat16)
    pieces = scaled.reshape(layers, n_col, width // n_col, width)
    arrived = lax.all_to_all(pieces, "col", split_axis=1, concat_axis=1, tiled=True)
    ordered = pick_along(arrived, inverse, 1)
    split = ordered.reshape(layers, n_col, n_row, width // (n_col * n_row), width)
    landed = lax.all_to_all(split, "row", split_axis=2, concat_axis=2, tiled=True)
    delta = outer - jnp.sum(landed.astype(jnp.float32), axis=2)
    moment_new = 0.9 * moment + delta
    outer_new = outer - 0.7 * (delta + 0.9 * moment_new)
    whole = lax.all_gather(outer_new.astype(jnp.bfloat16), "row", axis=2, tiled=True)
    chosen = pick_along(whole, my_row, 1)
    returned = lax.all_to_all(chosen, "col", split_axis=1, concat_axis=1, tiled=True)
    state = tokens.astype(jnp.float32)
    for layer in range(layers):
        scale = lax.rsqrt(jnp.mean(state * state, axis=-1, keepdims=True) + 1e-06)
        normed = (state * scale).astype(jnp.bfloat16)
        mixed = jnp.dot(normed, params[layer], preferred_element_type=jnp.float32)
        state = state + jax.nn.gelu(mixed, approximate=False)
    return returned, outer_new, moment_new, state.astype(jnp.bfloat16)


def on_device(tokens, local_params, outer_params, momentum, table, counts):
    n_col = table.shape[1]
    params = local_params[0, 0]
    layers, width = params.shape[0], params.shape[-1]
    outer = outer_params.reshape(layers, n_col, -1, width)
    moment = momentum.reshape(layers, n_col, -1, width)
    fits = outer.shape[2] % 16 == 0 and width % (PARTS * BLOCK) == 0 and tokens.shape[2] % 16 == 0
    run = with_kernel if fits else with_collectives
    returned, outer_new, moment_new, hidden = run(tokens[0, 0], params, outer, moment, table, counts)
    return (
        returned.reshape(local_params.shape),
        outer_new.reshape(outer_params.shape),
        moment_new.reshape(momentum.shape),
        hidden[None, None],
    )


def solution(mesh):
    return jax.shard_map(
        on_device,
        mesh=mesh,
        in_specs=(
            P("row", "col", None, None),
            P("row", "col", None, None, None),
            P(None, None, "col", "row", None, None),
            P(None, None, "col", "row", None, None),
            P(),
            P(),
        ),
        out_specs=(
            P("row", "col", None, None, None),
            P(None, None, "col", "row", None, None),
            P(None, None, "col", "row", None, None),
            P("row", "col", None, None),
        ),
        check_vma=False,
    )
```

```python
import functools

import jax
import jax.numpy as jnp
from jax import lax
from jax.experimental import pallas as pl
from jax.experimental.pallas import tpu as pltpu
from jax.sharding import PartitionSpec as P

MESH = pl.DeviceIdType.MESH
BLOCK = 256
PARTS = 2
TILE = 192


def round_kernel(
    n_row, n_col, tokens_in, params_in, source, outer_in, moment_in, table, counts,
    path, outer_out, moment_out, hidden_out,
    tokens, params, outer, moment, outer_new, moment_new, hidden,
    weights, landed, own, pair_out, pair_in, z_out, z_in, chosen, state, normed,
    in_send, in_recv, pair_send, pair_recv, z_send, z_recv, b_send, b_recv, f_send, f_recv,
    ret_send, ret_recv, here_sem, load_sem, store_sem, *spread,
):
    row, col = lax.axis_index("row"), lax.axis_index("col")
    layers, width = params.shape[0], params.shape[2]
    part = width // PARTS
    blocks = part // BLOCK
    chunks = [(layer, p) for layer in range(layers) for p in range(PARTS)]
    n_chunks = len(chunks)
    half = n_col // 2
    fresh_own, near, far = (spread[i * n_chunks : (i + 1) * n_chunks] for i in range(3))
    pair = col + 1 - 2 * lax.rem(col, 2)

    barrier = pltpu.get_barrier_semaphore()
    for d in range(1, n_row):
        pl.semaphore_signal(barrier, inc=1, device_id=(lax.rem(row + d, n_row), col), device_id_type=MESH)
    for d in range(1, n_col):
        pl.semaphore_signal(barrier, inc=1, device_id=(row, lax.rem(col + d, n_col)), device_id_type=MESH)
    pl.semaphore_wait(barrier, n_row + n_col - 2)

    def cols(k):
        return pl.ds(chunks[k][1] * part, part)

    def remote(src, dst, send, recv, to):
        return pltpu.make_async_remote_copy(
            src_ref=src, dst_ref=dst, send_sem=send, recv_sem=recv, device_id=to, device_id_type=MESH
        )

    def in_copy(k, slot, to):
        src = source.at[chunks[k][0], :, to, :, cols(k)]
        return remote(src, landed.at[k, slot], in_send.at[k, to], in_recv.at[k, slot], (to, col))

    def in_own(k):
        return pltpu.make_async_copy(source.at[chunks[k][0], :, row, :, cols(k)], landed.at[k, row], here_sem.at[0, k])

    def pair_copy(k):
        return remote(pair_out.at[k], pair_in.at[k], pair_send.at[k], pair_recv.at[k], (row, pair))

    def ahead(d):
        return (row, lax.rem(col + 2 * d, n_col))

    def z_copy(k, d):
        return remote(z_out.at[k, d - 1], z_in.at[k, d - 1], z_send.at[k, d], z_recv.at[k, d], ahead(d))

    def b_copy(k, d):
        return remote(fresh_own[k], near[k].at[d - 1], b_send.at[k, d], b_recv.at[k, d], ahead(d))

    def f_copy(k, d):
        block = near[k].at[d - 1] if d else fresh_own[k]
        return remote(block, far[k].at[d], f_send.at[k, d], f_recv.at[k, d], (row, pair))

    def ret_copy(k, slot, to):
        dst = path.at[chunks[k][0], :, slot, :, cols(k)]
        return remote(chosen.at[k, to], dst, ret_send.at[k, to], ret_recv.at[k, slot], (to, col))

    def ret_own(k):
        return pltpu.make_async_copy(chosen.at[k, row], path.at[chunks[k][0], :, row, :, cols(k)], here_sem.at[1, k])

    def others(me, n):
        return [lax.rem(me + d, n) for d in range(1, n)]

    loads = [
        pltpu.make_async_copy(src, dst, load_sem.at[i])
        for i, (src, dst) in enumerate(
            [(tokens_in, tokens), (params_in, params), (outer_in, outer), (moment_in, moment)]
        )
    ]

    for k in range(n_chunks):
        in_own(k).start()
        for to in others(row, n_row):
            in_copy(k, row, to).start()
        if k == 0:
            for load in loads:
                load.start()

    def fill_weight(i, carry):
        module = table[i, col]

        def add(at, total):
            r, c = at // n_col, at % n_col
            return total + jnp.where(table[r, c] == module, counts[r, c], 0)

        total = lax.fori_loop(0, n_row * n_col, add, jnp.int32(0))
        shape = weights.shape[1:]
        weights[i] = jnp.full(shape, counts[i, col].astype(jnp.float32)) / jnp.full(shape, total.astype(jnp.float32))
        return carry

    lax.fori_loop(0, n_row, fill_weight, 0)

    def micro(start, size):
        rows = pl.ds(start, size)
        state[rows] = tokens[rows].astype(jnp.float32)
        for layer in range(layers):
            def norm(b, carry):
                few = pl.ds(pl.multiple_of(start + b * 16, 16), 16)
                value = state[few]
                scale = lax.rsqrt(jnp.mean(value * value, axis=-1, keepdims=True) + 1e-06)
                normed[few] = (value * scale).astype(jnp.bfloat16)
                return carry

            lax.fori_loop(0, size // 16, norm, 0)

            def mix(b, carry):
                at = pl.ds(pl.multiple_of(b * BLOCK, BLOCK), BLOCK)
                mixed = jnp.dot(normed[rows], params[layer, :, at], preferred_element_type=jnp.float32)
                state[rows, at] += 0.5 * mixed * (1.0 + lax.erf(mixed * (0.5**0.5)))
                return carry

            lax.fori_loop(0, width // BLOCK, mix, 0)
        hidden[rows] = state[rows].astype(jnp.bfloat16)

    def reduce(k):
        in_own(k).wait()
        for frm in others(row, n_row):
            in_copy(k, frm, frm).wait_recv()

        def sums_of(to, at):
            sums = [jnp.zeros((landed.shape[3], BLOCK), jnp.float32) for _ in range(n_col)]
            for i in range(n_row):
                term = (weights[i] * landed[k, i, to, :, at].astype(jnp.float32)).astype(jnp.bfloat16)
                term = term.astype(jnp.float32)
                module = table[i, col]
                for m in range(n_col):
                    sums[m] += term * jnp.where(module == m, 1.0, 0.0).astype(jnp.float32)
            return sums

        for d in range(half):

            def away(b, carry, d=d):
                at = pl.ds(pl.multiple_of(b * BLOCK, BLOCK), BLOCK)
                for m, value in enumerate(sums_of(lax.rem(pair + 2 * d, n_col), at)):
                    pair_out[k, d, m, :, at] = value.astype(jnp.bfloat16)
                return carry

            lax.fori_loop(0, blocks, away, 0)
        pair_copy(k).start()

        for d in range(half):

            def kept(b, carry, d=d):
                at = pl.ds(pl.multiple_of(b * BLOCK, BLOCK), BLOCK)
                for m, value in enumerate(sums_of(lax.rem(col + 2 * d, n_col), at)):
                    own[k, d, m, :, at] = value
                return carry

            lax.fori_loop(0, blocks, kept, 0)

    def halfway(k):
        pair_copy(k).wait_recv()
        for d in range(1, half):

            def block(m, carry, d=d):
                z_out[k, d - 1, m] = (own[k, d, m] + pair_in[k, d, m].astype(jnp.float32)).astype(jnp.bfloat16)
                return carry

            lax.fori_loop(0, n_col, block, 0)
            z_copy(k, d).start()

    def update(k):
        layer, p = chunks[k]
        for d in range(1, half):
            z_copy(k, d).wait_recv()

        def block(b, carry):
            at = pl.ds(pl.multiple_of(b * BLOCK, BLOCK), BLOCK)
            whole = pl.ds(pl.multiple_of(p * part + b * BLOCK, BLOCK), BLOCK)
            for m in range(n_col):
                average = own[k, 0, m, :, at] + pair_in[k, 0, m, :, at].astype(jnp.float32)
                for d in range(1, half):
                    average += z_in[k, d - 1, m, :, at].astype(jnp.float32)
                old = outer[layer, m, :, whole]
                delta = old - average
                fresh = 0.9 * moment[layer, m, :, whole] + delta
                new = old - 0.7 * (delta + 0.9 * fresh)
                moment_new[layer, m, :, whole] = fresh
                outer_new[layer, m, :, whole] = new
                fresh_own[k][m, :, at] = new.astype(jnp.bfloat16)
            return carry

        lax.fori_loop(0, blocks, block, 0)
        for d in range(1, half):
            b_copy(k, d).start()
        f_copy(k, 0).start()

    def forward(k):
        for d in range(1, half):
            b_copy(k, d).wait_recv()
            f_copy(k, d).start()

    def give(k):
        for h in range(half):
            f_copy(k, h).wait_recv()

        for d in [*range(1, n_row), 0]:
            to = lax.rem(row + d, n_row)
            module = table[to, col]
            for back in range(half):
                apart = n_col - 2 * back
                chosen[k, to, lax.rem(col + apart, n_col)] = near[k][back - 1, module] if back else fresh_own[k][module]
                chosen[k, to, lax.rem(pair + apart, n_col)] = far[k][back, module]
            if d:
                ret_copy(k, row, to).start()
            else:
                ret_own(k).start()

    stores = [
        pltpu.make_async_copy(src, dst, store_sem.at[i])
        for i, (src, dst) in enumerate([(outer_new, outer_out), (moment_new, moment_out), (hidden, hidden_out)])
    ]
    tiles = [(s, min(TILE, tokens.shape[0] - s)) for s in range(0, tokens.shape[0], TILE)]
    for step in range(max(n_chunks + 2, len(tiles))):
        if step < n_chunks:
            reduce(step)
        if 1 <= step < n_chunks + 1:
            if step == 1:
                loads[2].wait()
                loads[3].wait()
            update(step - 1)
            if step == n_chunks:
                stores[0].start()
                stores[1].start()
        if 2 <= step < n_chunks + 2:
            give(step - 2)
        if step < len(tiles):
            if step == 0:
                loads[0].wait()
                loads[1].wait()
            micro(*tiles[step])
            if step == len(tiles) - 1:
                stores[2].start()
        if step < n_chunks:
            halfway(step)
        if 1 <= step < n_chunks + 1:
            forward(step - 1)

    for k in range(n_chunks):
        pair_copy(k).wait_send()
        for d in range(half):
            if d:
                z_copy(k, d).wait_send()
                b_copy(k, d).wait_send()
            f_copy(k, d).wait_send()
        ret_own(k).wait()
        for at in others(row, n_row):
            in_copy(k, row, at).wait_send()
            ret_copy(k, row, at).wait_send()
    for k in range(n_chunks):
        for at in others(row, n_row):
            ret_copy(k, at, at).wait_recv()
    for store in stores:
        store.wait()


def with_kernel(tokens, params, outer, moment, table, counts):
    n_row, n_col = table.shape
    layers, width = params.shape[0], params.shape[-1]
    piece = outer.shape[2]
    part = width // PARTS
    n_chunks = layers * PARTS
    half = n_col // 2
    source = params.reshape(layers, n_col, n_row, piece, width)
    smem = pl.BlockSpec(memory_space=pltpu.SMEM)
    hbm = pl.BlockSpec(memory_space=pl.ANY)
    n_tokens = tokens.shape[0]
    flops = 2 * layers * n_tokens * width * width
    by_row = pltpu.SemaphoreType.DMA((n_chunks, n_row))
    by_half = pltpu.SemaphoreType.DMA((n_chunks, half))
    by_chunk = pltpu.SemaphoreType.DMA((n_chunks,))
    return pl.pallas_call(
        functools.partial(round_kernel, n_row, n_col),
        out_shape=(
            jax.ShapeDtypeStruct(source.shape, jnp.bfloat16),
            jax.ShapeDtypeStruct(outer.shape, jnp.float32),
            jax.ShapeDtypeStruct(outer.shape, jnp.float32),
            jax.ShapeDtypeStruct(tokens.shape, jnp.bfloat16),
        ),
        in_specs=[hbm, hbm, hbm, hbm, hbm, smem, smem],
        out_specs=(hbm, hbm, hbm, hbm),
        scratch_shapes=[
            pltpu.VMEM(tokens.shape, jnp.bfloat16),
            pltpu.VMEM(params.shape, jnp.bfloat16),
            pltpu.VMEM(outer.shape, jnp.float32),
            pltpu.VMEM(outer.shape, jnp.float32),
            pltpu.VMEM(outer.shape, jnp.float32),
            pltpu.VMEM(outer.shape, jnp.float32),
            pltpu.VMEM(tokens.shape, jnp.bfloat16),
            pltpu.VMEM((n_row, 1, BLOCK), jnp.float32),
            pltpu.VMEM((n_chunks, n_row, n_col, piece, part), jnp.bfloat16),
            pltpu.VMEM((n_chunks, half, n_col, piece, part), jnp.float32),
            pltpu.VMEM((n_chunks, half, n_col, piece, part), jnp.bfloat16),
            pltpu.VMEM((n_chunks, half, n_col, piece, part), jnp.bfloat16),
            pltpu.VMEM((n_chunks, half, n_col, piece, part), jnp.bfloat16),
            pltpu.VMEM((n_chunks, half, n_col, piece, part), jnp.bfloat16),
            pltpu.VMEM((n_chunks, n_row, n_col, piece, part), jnp.bfloat16),
            pltpu.VMEM((n_tokens, width), jnp.float32),
            pltpu.VMEM((n_tokens, width), jnp.bfloat16),
            by_row, by_row, by_chunk, by_chunk, by_half, by_half, by_half, by_half, by_half, by_half, by_row, by_row,
            pltpu.SemaphoreType.DMA((2, n_chunks)),
            pltpu.SemaphoreType.DMA((4,)),
            pltpu.SemaphoreType.DMA((3,)),
            *[pltpu.VMEM((n_col, piece, part), jnp.bfloat16) for _ in range(n_chunks)],
            *[pltpu.VMEM((max(half - 1, 1), n_col, piece, part), jnp.bfloat16) for _ in range(n_chunks)],
            *[pltpu.VMEM((half, n_col, piece, part), jnp.bfloat16) for _ in range(n_chunks)],
        ],
        compiler_params=pltpu.CompilerParams(
            collective_id=0, has_side_effects=True, vmem_limit_bytes=52 * 1024 * 1024
        ),
        cost_estimate=pl.CostEstimate(flops=flops, bytes_accessed=20 * 2**20, transcendentals=0),
    )(tokens, params, source, outer, moment, table, counts)


def pick_along(array, index, axis):
    parts = [lax.dynamic_index_in_dim(array, index[m], axis) for m in range(index.shape[0])]
    return jnp.concatenate(parts, axis=axis)


def with_collectives(tokens, params, outer, moment, table, counts):
    n_row, n_col = table.shape
    layers, width = params.shape[0], params.shape[-1]
    ids = jnp.arange(n_col, dtype=jnp.int32)
    matches = (table[:, :, None] == ids[None, None, :]).astype(jnp.float32)
    totals = jnp.sum(counts.astype(jnp.float32)[:, :, None] * matches, axis=(0, 1))
    my_row = lax.dynamic_index_in_dim(table, lax.axis_index("row"), 0, keepdims=False)
    count_row = lax.dynamic_index_in_dim(counts, lax.axis_index("row"), 0, keepdims=False)
    my_module = lax.dynamic_index_in_dim(my_row, lax.axis_index("col"), 0, keepdims=False)
    my_count = lax.dynamic_index_in_dim(count_row, lax.axis_index("col"), 0, keepdims=False)
    share = my_count.astype(jnp.float32) / jnp.sum(totals * (ids == my_module).astype(jnp.float32))
    inverse = jnp.sum(ids[:, None] * (my_row[:, None] == ids[None, :]).astype(jnp.int32), axis=0)
    scaled = (share * params.astype(jnp.float32)).astype(jnp.bfloat16)
    pieces = scaled.reshape(layers, n_col, width // n_col, width)
    arrived = lax.all_to_all(pieces, "col", split_axis=1, concat_axis=1, tiled=True)
    ordered = pick_along(arrived, inverse, 1)
    split = ordered.reshape(layers, n_col, n_row, width // (n_col * n_row), width)
    landed = lax.all_to_all(split, "row", split_axis=2, concat_axis=2, tiled=True)
    delta = outer - jnp.sum(landed.astype(jnp.float32), axis=2)
    moment_new = 0.9 * moment + delta
    outer_new = outer - 0.7 * (delta + 0.9 * moment_new)
    whole = lax.all_gather(outer_new.astype(jnp.bfloat16), "row", axis=2, tiled=True)
    chosen = pick_along(whole, my_row, 1)
    returned = lax.all_to_all(chosen, "col", split_axis=1, concat_axis=1, tiled=True)
    state = tokens.astype(jnp.float32)
    for layer in range(layers):
        scale = lax.rsqrt(jnp.mean(state * state, axis=-1, keepdims=True) + 1e-06)
        normed = (state * scale).astype(jnp.bfloat16)
        mixed = jnp.dot(normed, params[layer], preferred_element_type=jnp.float32)
        state = state + jax.nn.gelu(mixed, approximate=False)
    return returned, outer_new, moment_new, state.astype(jnp.bfloat16)


def on_device(tokens, local_params, outer_params, momentum, table, counts):
    n_col = table.shape[1]
    params = local_params[0, 0]
    layers, width = params.shape[0], params.shape[-1]
    outer = outer_params.reshape(layers, n_col, -1, width)
    moment = momentum.reshape(layers, n_col, -1, width)
    fits = n_col % 2 == 0 and outer.shape[2] % 16 == 0 and width % (PARTS * BLOCK) == 0 and tokens.shape[2] % 16 == 0
    run = with_kernel if fits else with_collectives
    returned, outer_new, moment_new, hidden = run(tokens[0, 0], params, outer, moment, table, counts)
    return (
        returned.reshape(local_params.shape),
        outer_new.reshape(outer_params.shape),
        moment_new.reshape(momentum.shape),
        hidden[None, None],
    )


def solution(mesh):
    return jax.shard_map(
        on_device,
        mesh=mesh,
        in_specs=(
            P("row", "col", None, None),
            P("row", "col", None, None, None),
            P(None, None, "col", "row", None, None),
            P(None, None, "col", "row", None, None),
            P(),
            P(),
        ),
        out_specs=(
            P("row", "col", None, None, None),
            P(None, None, "col", "row", None, None),
            P(None, None, "col", "row", None, None),
            P("row", "col", None, None),
        ),
        check_vma=False,
    )
```
